32 devices in a mesh: groups: 2 (over x), ep: 16 (over z, y, core).
Axes of the slice: x: 2, y: 2, z: 4, core: 2. Of those that a mesh axis runs over, the one named last changes fastest.
Arguments:
- tokens: bfloat16 [2048, 7168], P(('groups', 'ep')), parts along dimension 0, may hold values from -6 to 6
- expert_ids: int32 [2048, 2], P(('groups', 'ep')), parts along dimension 0, may hold values from 0 to 7, all different within a row; in each aligned block of 64 rows (0 to 63, 64 to 127, ...) at most 24 rows name the same one
- gate_scale: float32 [2048, 2], P(('groups', 'ep')), parts along dimension 0, may hold values from 0.2 to 1
- gate_weight: bfloat16 [16, 7168, 512], P('ep'), may hold values from -0.0625 to 0.0625
- up_weight: bfloat16 [16, 7168, 512], P('ep'), may hold values from -0.0625 to 0.0625
- down_weight: bfloat16 [16, 512, 7168], P('ep'), may hold values from -0.1875 to 0.1875
Outputs:
- mixed: bfloat16 [2048, 7168], P(('groups', 'ep')), parts along dimension 0
The draws below stay inside these ranges and needn't reach their ends.
There are 2 independent parts, one for each index of `groups`. The reference program is written for one: setup_inputs(seed, part) draws one part's arguments, and reference() takes and returns one part's arrays. A program takes and returns all parts, laid end to end along the dimension named above; an argument that names none is the same for every part. Nothing has to cross between parts.
Inputs may be any that keep to these rules, and one draw needn't show every extreme that they name: `expert_ids`: each row names 2 different experts. Among the 64 rows of one device no expert is named by more than 24 rows, and in every draw some expert is named by exactly 24 rows of some device.
All inputs are finite; a program needn't handle non-finite values.
Results may differ from the reference program's by a relative error of at most 0.0058.
Values may be sent and summed in bfloat16 or wider, within the bound.
A program may use at most 128 MiB of HBM per device.

```python
import math
import jax
import jax.numpy as jnp
import numpy as np
from jax import lax

D = 7168
FF = 1024
SPLIT = 2
TOP = 2
TOK_DEV = 64
FF_DEV = 512
EXPERTS = 8
CAP = 24
TOKENS = 1024
N_EP = 16


def block_scale(key, dims, shards, low, top_value):
    def one(dim, blocks):
        draws = jax.random.uniform(jax.random.fold_in(jax.random.fold_in(key, 6), dim), (blocks,), jnp.float32, low / len(shards), top_value / len(shards))
        return jnp.repeat(jnp.exp(draws), dims[dim] // blocks).reshape((-1,) + (1,) * (len(dims) - dim - 1))

    loudness = one(*shards[0])
    for cut in shards[1:]:
        loudness = loudness * one(*cut)
    return loudness


def deal_out(own_key, own, number, rows, count, top, limit, slope):
    order = jax.random.permutation(own_key, count)
    packed, usual = load_shares(count, rows * top, limit, slope, True), load_shares(count, rows * top, limit, slope, False)
    places = jnp.arange(count)

    def named(lengths, offset_by):
        used = int((lengths > 0).sum())
        fixed = max(1, used // 4)
        moved = fixed + (places - fixed + offset_by * (used - fixed)) % max(1, count - fixed)
        return jnp.zeros((count,), jnp.int32).at[order[jnp.where(places < fixed, places, moved)]].set(jnp.asarray(lengths, jnp.int32))

    lengths = jnp.where(number % 4 == 0, named(packed, number // 4), named(usual, number - number // 4 - 1))
    mixed = jax.random.permutation(jax.random.fold_in(own, 3), count)
    donor, receiver = mixed[0:count // 2 * 2:2], mixed[1:count // 2 * 2:2]
    margin = jnp.minimum(lengths[donor] - 1, limit - lengths[receiver]) // 2
    margin = jnp.where((donor == order[0]) | (receiver == order[0]) | (lengths[receiver] == 0), 0, jnp.maximum(margin, 0))
    moved = jax.random.randint(jax.random.fold_in(own, 4), (count // 2,), 0, 1 << 20) % (margin + 1)
    lengths = lengths.at[donor].add(-moved).at[receiver].add(moved)
    labels = jnp.searchsorted(jnp.cumsum(lengths), jnp.arange(rows * top), side="right").astype(jnp.int32)
    grid = labels.reshape(top, rows).T
    grid = grid[jax.random.permutation(jax.random.fold_in(own, 1), rows)]
    offset_by = jax.random.randint(jax.random.fold_in(own, 2), (rows, 1), 0, top)
    return jnp.take_along_axis(grid, (jnp.arange(top)[None, :] + offset_by) % top, axis=1)


def load_shares(count, total, reach, lean, full):
    loads = [(1 << 20) // math.isqrt(rank ** lean) + 1 for rank in range(1, count + 1)]
    largest = reach if full else min(reach, max(-(-total // count), total * loads[0] // sum(loads)))
    least = 1 if total - largest >= count - 1 else 0
    counts, spare = [largest] + [least] * (count - 1), total - largest - least * (count - 1)
    while spare > 0:
        movable = [i for i in range(1, count) if counts[i] < largest] or [i for i in range(1, count) if counts[i] < reach]
        mass, budget = sum([loads[i] for i in movable]), spare
        for i in movable:
            addition = min(reach - counts[i], max(1, budget * loads[i] // mass), spare)
            counts[i] = counts[i] + addition
            spare = spare - addition
    return np.array(counts)


def noise(own_key, dims, spread, limit, split=(), kind=jnp.bfloat16):
    drawn = spread * jax.random.normal(own_key, dims, jnp.float32)
    if split:
        drawn = drawn * block_scale(own_key, dims, split, -0.22, 0.18)
    return jnp.clip(drawn, -limit, limit).astype(kind)


def setup_inputs(seed: int = 0, part: int = 0) -> dict:
    splits = jax.random.split(jax.random.key(seed), 7)
    part_keys = jax.random.split(jax.random.fold_in(splits[6], part), 7)
    tokens = noise(part_keys[0], (TOKENS, D), 1.0, 6.0, ((0, 16),))
    expert_ids_keys = jax.random.split(jax.random.fold_in(part_keys[1], 1), TOKENS // TOK_DEV)
    expert_ids_turns = jax.random.permutation(jax.random.fold_in(part_keys[1], 3), TOKENS // TOK_DEV)
    expert_ids = jax.vmap(lambda own, number: deal_out(jax.random.fold_in(part_keys[1], 2), own, number, TOK_DEV, EXPERTS, TOP, CAP, 2))(expert_ids_keys, expert_ids_turns).reshape((TOKENS, TOP))
    gate_scale = jnp.clip(0.2 + 0.8 * jax.random.uniform(part_keys[2], (TOKENS, TOP), jnp.float32) ** block_scale(part_keys[2], (TOKENS, TOP), ((0, 16),), -0.2, 0.2), 0.2, 1.0)
    gate_weight = noise(splits[3], (N_EP, D, FF_DEV), D ** -0.5, 0.0625, ((0, 16),))
    up_weight = noise(splits[4], (N_EP, D, FF_DEV), D ** -0.5, 0.0625, ((0, 16),))
    down_weight = noise(splits[5], (N_EP, FF_DEV, D), FF ** -0.5, 0.1875, ((0, 16),))
    return dict(tokens=tokens, expert_ids=expert_ids, gate_scale=gate_scale, gate_weight=gate_weight, up_weight=up_weight, down_weight=down_weight)


def expert_apply(operands):
    block_rows, w_gate, w_up, w_down = operands
    gate_act = jnp.dot(block_rows, w_gate, preferred_element_type=jnp.float32)
    up_act = jnp.dot(block_rows, w_up, preferred_element_type=jnp.float32)
    hidden = (jax.nn.silu(gate_act) * up_act).astype(jnp.bfloat16)
    return jnp.dot(hidden, w_down, preferred_element_type=jnp.float32).astype(jnp.bfloat16)


def reference(tokens, expert_ids, gate_scale, gate_weight, up_weight, down_weight):
    flat_ids = expert_ids.reshape(N_EP, TOK_DEV * TOP).astype(jnp.int32)
    one_hot = (flat_ids[:, :, None] == jnp.arange(EXPERTS, dtype=jnp.int32)[None, None, :]).astype(jnp.int32)
    before = jnp.cumsum(one_hot, axis=1) - one_hot
    slot_index = jnp.sum(before * one_hot, axis=2).astype(jnp.int32)
    source = jnp.arange(N_EP, dtype=jnp.int32)[:, None]
    position = (flat_ids * (N_EP * CAP) + source * CAP + slot_index).reshape(-1).astype(jnp.int32)
    row_index = (jnp.arange(TOKENS * TOP, dtype=jnp.int32) // TOP).astype(jnp.int32)
    total_slots = EXPERTS * N_EP * CAP
    source_row = jnp.zeros((total_slots,), jnp.int32).at[position].set(row_index)
    filled = jnp.zeros((total_slots,), jnp.bfloat16).at[position].set(jnp.ones((TOKENS * TOP,), jnp.bfloat16))
    buffer = (tokens[source_row] * filled[:, None]).reshape(EXPERTS, N_EP * CAP, D)
    w_gate = gate_weight.reshape(EXPERTS, SPLIT, D, FF_DEV).transpose(0, 2, 1, 3).reshape(EXPERTS, D, FF)
    w_up = up_weight.reshape(EXPERTS, SPLIT, D, FF_DEV).transpose(0, 2, 1, 3).reshape(EXPERTS, D, FF)
    w_down = down_weight.reshape(EXPERTS, FF, D)
    results = lax.map(expert_apply, (buffer, w_gate, w_up, w_down))
    picked = results.reshape(total_slots, D)[position].reshape(TOKENS, TOP, D).astype(jnp.float32)
    mixed = jnp.sum(gate_scale.astype(jnp.float32)[:, :, None] * picked, axis=1)
    return mixed.astype(jnp.bfloat16)
```

```python
import functools

import jax
import jax.numpy as jnp
from jax import lax
from jax.experimental import pallas as pl
from jax.experimental.pallas import tpu as pltpu
from jax.sharding import PartitionSpec as P

CHUNKS = 8
BF16, F32 = jnp.bfloat16, jnp.float32


def layer_kernel(
    n_ep, cap, ids_ref, ids_t_ref, scale_ref, tok_ref, wg_hbm, wu_hbm, wd_hbm, out_ref,
    send, recv, ret, res, wg, wu, wd, gate_acc, up_acc, hid, mix,
    w_sem, wd_send, wd_recv, send_sem, own_sem, pair_sem, recv_sem, fwd_sem,
    hid_send, hid_recv, ret_sem, res_sem,
):
    me = lax.axis_index("ep")
    chip = me // 2
    core = me % 2
    partner = chip * 2 + 1 - core
    experts = n_ep // 2
    rows, width = tok_ref.shape
    w = width // CHUNKS
    per_core = CHUNKS // 2
    half = width // 2

    def remote(src, dst, ssem, rsem, dev):
        return pltpu.make_async_remote_copy(
            src_ref=src, dst_ref=dst, send_sem=ssem, recv_sem=rsem,
            device_id={"ep": dev}, device_id_type=pl.DeviceIdType.MESH,
        )

    def chip_at(d):
        return lax.rem(chip + d, experts)

    my_cols = pl.ds(pl.multiple_of(core * half, 128), half)
    pair_cols = pl.ds(pl.multiple_of((1 - core) * half, 128), half)
    load_g = pltpu.make_async_copy(wg_hbm.at[0], wg, w_sem.at[0])
    load_u = pltpu.make_async_copy(wu_hbm.at[0], wu, w_sem.at[1])
    load_d = pltpu.make_async_copy(wd_hbm.at[0, :, my_cols], wd.at[core], w_sem.at[2])
    load_g.start()
    load_u.start()
    load_d.start()

    barrier = pltpu.get_barrier_semaphore()
    for i in range(1, n_ep):
        pl.semaphore_signal(
            barrier, inc=1, device_id={"ep": lax.rem(me + i, n_ep)},
            device_id_type=pl.DeviceIdType.MESH,
        )

    shape3 = (experts, cap, rows)
    block = lax.broadcasted_iota(jnp.int32, shape3, 0).reshape(experts * cap, rows)
    slot = lax.broadcasted_iota(jnp.int32, shape3, 1).reshape(experts * cap, rows)
    named = chip + block
    named = jnp.where(named >= experts, named - experts, named)
    hit = (ids_t_ref[0:1, :] == named) | (ids_t_ref[1:2, :] == named)
    r0 = lax.broadcasted_iota(jnp.int32, (rows, rows), 0)
    r1 = lax.broadcasted_iota(jnp.int32, (rows, rows), 1)
    upper = jnp.where(r0 < r1, 1.0, 0.0).astype(BF16)
    lower = jnp.where(r1 < r0, 1.0, 0.0).astype(BF16)
    hit_f = jnp.where(hit, 1.0, 0.0)
    before = jnp.dot(hit_f.astype(BF16), upper, preferred_element_type=F32)
    pick = jnp.where(before == slot.astype(F32), hit_f, 0.0).astype(BF16)

    pl.semaphore_wait(barrier, n_ep - 1)

    def dispatch(k, _):
        cols = pl.ds(pl.multiple_of(k * w, 128), w)
        picked = jnp.dot(pick, tok_ref[:, cols], preferred_element_type=F32)
        send[k] = picked.reshape(experts, cap, w).astype(BF16)
        for d in range(1, experts):
            remote(
                send.at[k, d], recv.at[k, 2 * (experts - d) + core], send_sem.at[k],
                recv_sem.at[k], chip_at(d) * 2 + k % 2,
            ).start()
        remote(
            send.at[k, 0], recv.at[k, core], send_sem.at[k], pair_sem.at[k], partner
        ).start()
        pltpu.make_async_copy(send.at[k, 0], recv.at[k, core], own_sem.at[k]).start()
        return 0

    lax.fori_loop(0, CHUNKS, dispatch, 0)

    give_d = remote(wd_hbm.at[0, :, pair_cols], wd.at[core], wd_send, wd_recv, partner)
    give_d.start()

    column = lax.broadcasted_iota(jnp.int32, (rows, experts * cap), 1)
    block2 = jnp.zeros_like(column)
    for i in range(1, experts):
        block2 = block2 + jnp.where(column >= i * cap, 1, 0)
    slot2 = column - block2 * cap
    named2 = chip + block2
    named2 = jnp.where(named2 >= experts, named2 - experts, named2)
    hit_a = ids_ref[:, 0:1] == named2
    hit_b = ids_ref[:, 1:2] == named2
    hit2 = jnp.where(hit_a | hit_b, 1.0, 0.0)
    before2 = jnp.dot(lower, hit2.astype(BF16), preferred_element_type=F32)
    scale = jnp.where(hit_a, scale_ref[:, 0:1], 0.0) + jnp.where(hit_b, scale_ref[:, 1:2], 0.0)
    scale = jnp.where(before2 == slot2.astype(F32), scale, 0.0)
    high = scale.astype(BF16)
    mix[0:rows] = high
    mix[rows:] = (scale - high.astype(F32)).astype(BF16)

    gate_acc[...] = jnp.zeros_like(gate_acc)
    up_acc[...] = jnp.zeros_like(up_acc)
    load_g.wait()
    load_u.wait()

    def arrived(ref, sem):
        pltpu.make_async_copy(ref, ref, sem).wait()

    def project(k):
        arrived(recv.at[k, core], own_sem.at[k])
        arrived(recv.at[k, 1 - core], pair_sem.at[k])
        x = recv[k].astype(F32).reshape(n_ep * cap, w).astype(BF16)
        depth = pl.ds(pl.multiple_of(k * w, 128), w)
        gate_acc[...] += jnp.dot(x, wg[depth, :], preferred_element_type=F32)
        up_acc[...] += jnp.dot(x, wu[depth, :], preferred_element_type=F32)

    def consume(p, _):
        mine = 2 * p + core
        other = 2 * p + 1 - core
        arrived(recv.at[mine, pl.ds(2, n_ep - 2)], recv_sem.at[mine])
        remote(
            recv.at[mine, pl.ds(2, n_ep - 2)], recv.at[mine, pl.ds(2, n_ep - 2)],
            fwd_sem.at[p], recv_sem.at[mine], partner,
        ).start()
        project(mine)
        arrived(recv.at[other, pl.ds(2, n_ep - 2)], recv_sem.at[other])
        project(other)
        return 0

    lax.fori_loop(0, per_core, consume, 0)

    g = gate_acc[...]
    hid[core] = (g / (1.0 + jnp.exp(-g)) * up_acc[...]).astype(BF16)
    swap = remote(hid.at[core], hid.at[core], hid_send, hid_recv, partner)
    swap.start()
    load_d.wait()
    arrived(wd.at[1 - core], wd_recv)
    arrived(hid.at[1 - core], hid_recv)

    def finish(j, _):
        cols = pl.ds(pl.multiple_of(j * w, 128), w)
        y = jnp.dot(hid[0], wd[0, :, cols], preferred_element_type=F32)
        y += jnp.dot(hid[1], wd[1, :, cols], preferred_element_type=F32)
        ret[j] = y.reshape(n_ep, cap, w).astype(BF16)
        k = core * per_core + j
        for d in range(1, experts):
            for b in range(2):
                remote(
                    ret.at[j, 2 * d + b], res.at[k, experts - d], ret_sem.at[j],
                    res_sem.at[k], chip_at(d) * 2 + b,
                ).start()
        remote(ret.at[j, 1 - core], res.at[k, 0], ret_sem.at[j], res_sem.at[k], partner).start()
        pltpu.make_async_copy(ret.at[j, core], res.at[k, 0], res_sem.at[k]).start()
        return 0

    lax.fori_loop(0, per_core, finish, 0)

    def combine(i, _):
        k = (i % 2) * per_core + i // 2
        arrived(res.at[k], res_sem.at[k])
        y = res[k].astype(F32).reshape(experts * cap, w).astype(BF16)
        both = jnp.dot(mix[...], y, preferred_element_type=F32)
        cols = pl.ds(pl.multiple_of(k * w, 128), w)
        out_ref[:, cols] = (both[0:rows] + both[rows:]).astype(BF16)
        return 0

    lax.fori_loop(0, CHUNKS, combine, 0)

    def drain(k, _):
        arrived(send.at[k], send_sem.at[k])
        return 0

    lax.fori_loop(0, CHUNKS, drain, 0)

    def drain_pairs(j, _):
        mine = 2 * j + core
        arrived(recv.at[mine, pl.ds(2, n_ep - 2)], fwd_sem.at[j])
        arrived(ret.at[j, pl.ds(0, n_ep - 1)], ret_sem.at[j])
        return 0

    lax.fori_loop(0, per_core, drain_pairs, 0)
    swap.wait_send()
    give_d.wait_send()


def shards(tokens, expert_ids, gate_scale, gate_weight, up_weight, down_weight):
    rows, width = tokens.shape
    top = expert_ids.shape[1]
    n_ep = lax.axis_size("ep")
    experts = n_ep // 2
    cap = 2 * (3 * rows * top // (4 * experts))
    cap = -(-cap // 8) * 8
    ff = gate_weight.shape[2]
    w = width // CHUNKS
    per_core = CHUNKS // 2
    vmem = pl.BlockSpec(memory_space=pltpu.VMEM)
    hbm = pl.BlockSpec(memory_space=pl.ANY)
    dma = pltpu.SemaphoreType.DMA
    total = n_ep * cap
    return pl.pallas_call(
        functools.partial(layer_kernel, n_ep, cap),
        out_shape=jax.ShapeDtypeStruct((rows, width), BF16),
        in_specs=[vmem, vmem, vmem, vmem, hbm, hbm, hbm],
        out_specs=vmem,
        scratch_shapes=[
            pltpu.VMEM((CHUNKS, experts, cap, w), BF16),
            pltpu.VMEM((CHUNKS, n_ep, cap, w), BF16),
            pltpu.VMEM((per_core, n_ep, cap, w), BF16),
            pltpu.VMEM((CHUNKS, experts, cap, w), BF16),
            pltpu.VMEM((width, ff), BF16),
            pltpu.VMEM((width, ff), BF16),
            pltpu.VMEM((2, ff, width // 2), BF16),
            pltpu.VMEM((total, ff), F32),
            pltpu.VMEM((total, ff), F32),
            pltpu.VMEM((2, total, ff), BF16),
            pltpu.VMEM((2 * rows, experts * cap), BF16),
            dma((3,)),
            dma,
            dma,
            dma((CHUNKS,)),
            dma((CHUNKS,)),
            dma((CHUNKS,)),
            dma((CHUNKS,)),
            dma((per_core,)),
            dma,
            dma,
            dma((per_core,)),
            dma((CHUNKS,)),
        ],
        compiler_params=pltpu.CompilerParams(
            collective_id=0, has_side_effects=True, vmem_limit_bytes=60 * 1024 * 1024
        ),
        cost_estimate=pl.CostEstimate(
            flops=6 * total * width * ff, bytes_accessed=6 * width * ff,
            transcendentals=total * ff,
        ),
    )(expert_ids, expert_ids.T, gate_scale, tokens, gate_weight, up_weight, down_weight)


def solution(mesh):
    in_specs = (
        P(("groups", "ep"), None),
        P(("groups", "ep"), None),
        P(("groups", "ep"), None),
        P("ep", None, None),
        P("ep", None, None),
        P("ep", None, None),
    )
    out_specs = P(("groups", "ep"), None)
    return jax.shard_map(shards, mesh=mesh, in_specs=in_specs, out_specs=out_specs, check_vma=False)
```

```python
import functools

import jax
import jax.numpy as jnp
from jax import lax
from jax.experimental import pallas as pl
from jax.experimental.pallas import tpu as pltpu
from jax.sharding import PartitionSpec as P

CHUNKS = 8
BF16, F32 = jnp.bfloat16, jnp.float32


def layer_kernel(
    n_ep, cap, ids_ref, scale_ref, tok_ref, wg_hbm, wu_hbm, wd_hbm, out_ref,
    send, recv, ret, res, raw, far_out, far_in, near, far_ids, far_scale,
    wg, wu, wd, gate_acc, up_acc, hid, picks, mixes,
    w_sem, wd_sem, meta_sem, raw_send, raw_recv, send_sem, own_sem, pair_sem, recv_sem,
    fwd_sem, hid_sem, ret_sem, res_sem, far_send, far_recv,
):
    me = lax.axis_index("ep")
    core = me % 2
    place = (me // 2) % (n_ep // 4)
    side = me // (n_ep // 2)
    span = n_ep // 4
    first = side * (n_ep // 2)
    partner = first + place * 2 + 1 - core
    twin = (1 - side) * (n_ep // 2) + place * 2 + core
    rows, width = tok_ref.shape
    w = width // CHUNKS
    per_core = CHUNKS // 2
    half = width // 2
    slots = span * cap

    def remote(src, dst, ssem, rsem, dev):
        return pltpu.make_async_remote_copy(
            src_ref=src, dst_ref=dst, send_sem=ssem, recv_sem=rsem,
            device_id={"ep": dev}, device_id_type=pl.DeviceIdType.MESH,
        )

    def near_device(d, b):
        return first + lax.rem(place + d, span) * 2 + b

    def columns(k):
        return pl.ds(pl.multiple_of(k * w, 128), w)

    def arrived(ref, sem):
        pltpu.make_async_copy(ref, ref, sem).wait()

    my_cols = pl.ds(pl.multiple_of(core * half, 128), half)
    pair_cols = pl.ds(pl.multiple_of((1 - core) * half, 128), half)
    load_g = pltpu.make_async_copy(wg_hbm.at[0], wg, w_sem.at[0])
    load_u = pltpu.make_async_copy(wu_hbm.at[0], wu, w_sem.at[1])
    load_d = pltpu.make_async_copy(wd_hbm.at[0, :, my_cols], wd.at[core], w_sem.at[2])
    load_g.start()
    load_u.start()
    load_d.start()

    barrier = pltpu.get_barrier_semaphore()
    for i in range(1, n_ep // 2):
        pl.semaphore_signal(
            barrier, inc=1, device_id={"ep": first + lax.rem(me + i, n_ep // 2)},
            device_id_type=pl.DeviceIdType.MESH,
        )
    pl.semaphore_signal(
        barrier, inc=1, device_id={"ep": twin}, device_id_type=pl.DeviceIdType.MESH
    )

    shape3 = (span, cap, rows)
    block = lax.broadcasted_iota(jnp.int32, shape3, 0).reshape(slots, rows)
    slot = lax.broadcasted_iota(jnp.int32, shape3, 1).reshape(slots, rows).astype(F32)
    named = place + block
    named = jnp.where(named >= span, named - span, named) + side * span
    r0 = lax.broadcasted_iota(jnp.int32, (rows, rows), 0)
    r1 = lax.broadcasted_iota(jnp.int32, (rows, rows), 1)
    earlier = jnp.where(r0 < r1, 1.0, 0.0).astype(BF16)
    unit = jnp.where(r0 == r1, 1.0, 0.0).astype(BF16)

    def plan(which, ids, scales):
        hit_a = ids[0:1, :] == named
        hit_b = ids[1:2, :] == named
        hit = jnp.where(hit_a | hit_b, 1.0, 0.0)
        before = jnp.dot(hit.astype(BF16), earlier, preferred_element_type=F32)
        hit = jnp.where(before == slot, hit, 0.0)
        picks[which] = hit.astype(BF16)
        scale = hit * jnp.where(hit_a, scales[0:1, :], scales[1:2, :])
        high = scale.astype(BF16)
        low = (scale - high.astype(F32)).astype(BF16)
        for i, term in enumerate((high, low)):
            mixes[which, i * rows:(i + 1) * rows] = lax.dot_general(
                unit, term, (((1,), (1,)), ((), ())), preferred_element_type=F32
            ).astype(BF16)

    pl.semaphore_wait(barrier, n_ep // 2)

    give_ids = remote(ids_ref, far_ids, meta_sem.at[0], meta_sem.at[1], twin)
    give_scale = remote(scale_ref, far_scale, meta_sem.at[2], meta_sem.at[3], twin)
    give_ids.start()
    give_scale.start()

    def cross(k, _):
        remote(tok_ref.at[:, columns(k)], raw.at[k], raw_send.at[k], raw_recv.at[k], twin).start()
        return 0

    lax.fori_loop(0, CHUNKS, cross, 0)
    plan(0, ids_ref, scale_ref)

    def spread(k, kind, x):
        picked = jnp.dot(picks[kind], x, preferred_element_type=F32)
        send[k, kind] = picked.reshape(span, cap, w).astype(BF16)
        for d in range(1, span):
            remote(
                send.at[k, kind, d], recv.at[k, 4 * (span - d) + 2 * core + kind],
                send_sem.at[k], recv_sem.at[k], near_device(d, k % 2),
            ).start()
        mine = recv.at[k, 2 * core + kind]
        remote(send.at[k, kind, 0], mine, send_sem.at[k], pair_sem.at[k], partner).start()
        pltpu.make_async_copy(send.at[k, kind, 0], mine, own_sem.at[k]).start()

    def relay(k):
        spread(k, 0, tok_ref[:, columns(k)])
        arrived(raw.at[k], raw_recv.at[k])
        spread(k, 1, raw[k])

    def project(k):
        arrived(recv.at[k, pl.ds(2 * core, 2)], own_sem.at[k])
        arrived(recv.at[k, pl.ds(2 - 2 * core, 2)], pair_sem.at[k])
        x = recv[k].astype(F32).reshape(n_ep * cap, w).astype(BF16)
        depth = columns(k)
        gate_acc[...] += jnp.dot(x, wg[depth, :], preferred_element_type=F32)
        up_acc[...] += jnp.dot(x, wu[depth, :], preferred_element_type=F32)

    def consume(p):
        mine = 2 * p + core
        other = 2 * p + 1 - core
        direct = recv.at[mine, pl.ds(4, n_ep - 4)]
        arrived(direct, recv_sem.at[mine])
        remote(direct, direct, fwd_sem.at[p], recv_sem.at[mine], partner).start()
        project(mine)
        arrived(recv.at[other, pl.ds(4, n_ep - 4)], recv_sem.at[other])
        project(other)

    gate_acc[...] = jnp.zeros_like(gate_acc)
    up_acc[...] = jnp.zeros_like(up_acc)
    give_ids.wait_recv()
    give_scale.wait_recv()
    plan(1, far_ids, far_scale)
    relay(0)
    relay(1)
    give_d = remote(wd_hbm.at[0, :, pair_cols], wd.at[core], wd_sem.at[0], wd_sem.at[1], partner)
    give_d.start()
    load_g.wait()
    load_u.wait()

    def step(p, _):
        relay(2 * p)
        relay(2 * p + 1)
        consume(p - 1)
        return 0

    lax.fori_loop(1, per_core, step, 0)
    consume(per_core - 1)

    g = gate_acc[...]
    hid[core] = (g / (1.0 + jnp.exp(-g)) * up_acc[...]).astype(BF16)
    swap = remote(hid.at[core], hid.at[core], hid_sem.at[0], hid_sem.at[1], partner)
    swap.start()
    load_d.wait()
    arrived(wd.at[1 - core], wd_sem.at[1])
    arrived(hid.at[1 - core], hid_sem.at[1])

    def finish(j, _):
        cols = columns(j)
        y = jnp.dot(hid[0], wd[0, :, cols], preferred_element_type=F32)
        y += jnp.dot(hid[1], wd[1, :, cols], preferred_element_type=F32)
        ret[j] = y.reshape(n_ep, cap, w).astype(BF16)
        k = core * per_core + j
        for d in range(1, span):
            for b in range(2):
                remote(
                    ret.at[j, pl.ds(4 * d + 2 * b, 2)], res.at[k, span - d], ret_sem.at[j],
                    res_sem.at[k], near_device(d, b),
                ).start()
        remote(
            ret.at[j, pl.ds(2 - 2 * core, 2)], res.at[k, 0], ret_sem.at[j], res_sem.at[k], partner
        ).start()
        pltpu.make_async_copy(
            ret.at[j, pl.ds(2 * core, 2)], res.at[k, 0], res_sem.at[k]
        ).start()
        return 0

    lax.fori_loop(0, per_core, finish, 0)

    def chunk(i):
        return (i % 2) * per_core + i // 2

    def mixed(k, kind):
        y = res[k, :, kind].astype(F32).reshape(slots, w).astype(BF16)
        both = jnp.dot(mixes[kind], y, preferred_element_type=F32)
        return both[0:rows] + both[rows:]

    def gather(i, _):
        k = chunk(i)
        arrived(res.at[k], res_sem.at[k])
        far_out[k] = mixed(k, 1).astype(BF16)
        remote(far_out.at[k], far_in.at[k], far_send.at[k], far_recv.at[k], twin).start()
        near[k] = mixed(k, 0)
        return 0

    lax.fori_loop(0, CHUNKS, gather, 0)

    def combine(i, _):
        k = chunk(i)
        arrived(far_in.at[k], far_recv.at[k])
        out_ref[:, columns(k)] = (near[k] + far_in[k].astype(F32)).astype(BF16)
        arrived(raw.at[k], raw_send.at[k])
        arrived(send.at[k], send_sem.at[k])
        arrived(far_out.at[k], far_send.at[k])
        return 0

    lax.fori_loop(0, CHUNKS, combine, 0)

    def drain_pairs(j, _):
        mine = 2 * j + core
        arrived(recv.at[mine, pl.ds(4, n_ep - 4)], fwd_sem.at[j])
        arrived(ret.at[j, pl.ds(0, n_ep - 2)], ret_sem.at[j])
        return 0

    lax.fori_loop(0, per_core, drain_pairs, 0)
    swap.wait_send()
    give_d.wait_send()
    give_ids.wait_send()
    give_scale.wait_send()


def shards(tokens, expert_ids, gate_scale, gate_weight, up_weight, down_weight):
    rows, width = tokens.shape
    top = expert_ids.shape[1]
    n_ep = lax.axis_size("ep")
    experts = n_ep // 2
    span = experts // 2
    cap = 2 * (3 * rows * top // (4 * experts))
    cap = -(-cap // 8) * 8
    ff = gate_weight.shape[2]
    w = width // CHUNKS
    per_core = CHUNKS // 2
    vmem = pl.BlockSpec(memory_space=pltpu.VMEM)
    hbm = pl.BlockSpec(memory_space=pl.ANY)
    dma = pltpu.SemaphoreType.DMA
    total = n_ep * cap
    return pl.pallas_call(
        functools.partial(layer_kernel, n_ep, cap),
        out_shape=jax.ShapeDtypeStruct((rows, width), BF16),
        in_specs=[vmem, vmem, vmem, hbm, hbm, hbm],
        out_specs=vmem,
        scratch_shapes=[
            pltpu.VMEM((CHUNKS, 2, span, cap, w), BF16),
            pltpu.VMEM((CHUNKS, n_ep, cap, w), BF16),
            pltpu.VMEM((per_core, n_ep, cap, w), BF16),
            pltpu.VMEM((CHUNKS, span, 2, cap, w), BF16),
            pltpu.VMEM((CHUNKS, rows, w), BF16),
            pltpu.VMEM((CHUNKS, rows, w), BF16),
            pltpu.VMEM((CHUNKS, rows, w), BF16),
            pltpu.VMEM((CHUNKS, rows, w), F32),
            pltpu.VMEM((top, rows), jnp.int32),
            pltpu.VMEM((top, rows), F32),
            pltpu.VMEM((width, ff), BF16),
            pltpu.VMEM((width, ff), BF16),
            pltpu.VMEM((2, ff, width // 2), BF16),
            pltpu.VMEM((total, ff), F32),
            pltpu.VMEM((total, ff), F32),
            pltpu.VMEM((2, total, ff), BF16),
            pltpu.VMEM((2, span * cap, rows), BF16),
            pltpu.VMEM((2, 2 * rows, span * cap), BF16),
            dma((3,)),
            dma((2,)),
            dma((4,)),
            dma((CHUNKS,)),
            dma((CHUNKS,)),
            dma((CHUNKS,)),
            dma((CHUNKS,)),
            dma((CHUNKS,)),
            dma((CHUNKS,)),
            dma((per_core,)),
            dma((2,)),
            dma((per_core,)),
            dma((CHUNKS,)),
            dma((CHUNKS,)),
            dma((CHUNKS,)),
        ],
        compiler_params=pltpu.CompilerParams(
            collective_id=0, has_side_effects=True, vmem_limit_bytes=60 * 1024 * 1024
        ),
        cost_estimate=pl.CostEstimate(
            flops=6 * total * width * ff, bytes_accessed=6 * width * ff,
            transcendentals=total * ff,
        ),
    )(expert_ids.T, gate_scale.T, tokens, gate_weight, up_weight, down_weight)


def solution(mesh):
    in_specs = (
        P(("groups", "ep"), None),
        P(("groups", "ep"), None),
        P(("groups", "ep"), None),
        P("ep", None, None),
        P("ep", None, None),
        P("ep", None, None),
    )
    out_specs = P(("groups", "ep"), None)
    return jax.shard_map(shards, mesh=mesh, in_specs=in_specs, out_specs=out_specs, check_vma=False)
```

```python
import functools

import jax
import jax.numpy as jnp
from jax import lax
from jax.experimental import pallas as pl
from jax.experimental.pallas import tpu as pltpu
from jax.sharding import PartitionSpec as P

CHUNKS = 14
BF16, F32 = jnp.bfloat16, jnp.float32


def layer_kernel(
    n_ep, cap, ids_ref, scale_ref, tok_ref, wg_hbm, wu_hbm, wd_hbm, out_ref,
    send, recv, ret, res, raw, far_out, far_in, near, far_ids, far_scale,
    wg, wu, wd, gate_acc, up_acc, hid, picks, mixes,
    w_sem, wd_sem, meta_sem, raw_send, raw_recv, send_sem, own_sem, pair_sem, recv_sem,
    fwd_sem, hid_sem, ret_sem, res_sem, far_send, far_recv,
):
    me = lax.axis_index("ep")
    core = me % 2
    place = (me // 2) % (n_ep // 4)
    side = me // (n_ep // 2)
    span = n_ep // 4
    first = side * (n_ep // 2)
    partner = first + place * 2 + 1 - core
    twin = (1 - side) * (n_ep // 2) + place * 2 + core
    rows, width = tok_ref.shape
    w = width // CHUNKS
    per_core = CHUNKS // 2
    half = width // 2
    slots = span * cap

    def remote(src, dst, ssem, rsem, dev):
        return pltpu.make_async_remote_copy(
            src_ref=src, dst_ref=dst, send_sem=ssem, recv_sem=rsem,
            device_id={"ep": dev}, device_id_type=pl.DeviceIdType.MESH,
        )

    def near_device(d, b):
        return first + lax.rem(place + d, span) * 2 + b

    def columns(k):
        return pl.ds(pl.multiple_of(k * w, 128), w)

    def arrived(ref, sem):
        pltpu.make_async_copy(ref, ref, sem).wait()

    my_cols = pl.ds(pl.multiple_of(core * half, 128), half)
    pair_cols = pl.ds(pl.multiple_of((1 - core) * half, 128), half)
    load_g = pltpu.make_async_copy(wg_hbm.at[0], wg, w_sem.at[0])
    load_u = pltpu.make_async_copy(wu_hbm.at[0], wu, w_sem.at[1])
    load_d = pltpu.make_async_copy(wd_hbm.at[0, :, my_cols], wd.at[core], w_sem.at[2])
    load_g.start()
    load_u.start()
    load_d.start()

    barrier = pltpu.get_barrier_semaphore()
    for i in range(1, n_ep // 2):
        pl.semaphore_signal(
            barrier, inc=1, device_id={"ep": first + lax.rem(me + i, n_ep // 2)},
            device_id_type=pl.DeviceIdType.MESH,
        )
    pl.semaphore_signal(
        barrier, inc=1, device_id={"ep": twin}, device_id_type=pl.DeviceIdType.MESH
    )

    shape3 = (span, cap, rows)
    block = lax.broadcasted_iota(jnp.int32, shape3, 0).reshape(slots, rows)
    slot = lax.broadcasted_iota(jnp.int32, shape3, 1).reshape(slots, rows).astype(F32)
    named = place + block
    named = jnp.where(named >= span, named - span, named) + side * span
    r0 = lax.broadcasted_iota(jnp.int32, (rows, rows), 0)
    r1 = lax.broadcasted_iota(jnp.int32, (rows, rows), 1)
    earlier = jnp.where(r0 < r1, 1.0, 0.0).astype(BF16)
    unit = jnp.where(r0 == r1, 1.0, 0.0).astype(BF16)

    def plan(which, ids, scales):
        hit_a = ids[0:1, :] == named
        hit_b = ids[1:2, :] == named
        hit = jnp.where(hit_a | hit_b, 1.0, 0.0)
        before = jnp.dot(hit.astype(BF16), earlier, preferred_element_type=F32)
        hit = jnp.where(before == slot, hit, 0.0)
        picks[which] = hit.astype(BF16)
        scale = hit * jnp.where(hit_a, scales[0:1, :], scales[1:2, :])
        high = scale.astype(BF16)
        low = (scale - high.astype(F32)).astype(BF16)
        for i, term in enumerate((high, low)):
            mixes[which, i * rows:(i + 1) * rows] = lax.dot_general(
                unit, term, (((1,), (1,)), ((), ())), preferred_element_type=F32
            ).astype(BF16)

    pl.semaphore_wait(barrier, n_ep // 2)

    give_ids = remote(ids_ref, far_ids, meta_sem.at[0], meta_sem.at[1], twin)
    give_scale = remote(scale_ref, far_scale, meta_sem.at[2], meta_sem.at[3], twin)
    give_ids.start()
    give_scale.start()

    def cross(k, _):
        remote(tok_ref.at[:, columns(k)], raw.at[k], raw_send.at[k], raw_recv.at[k], twin).start()
        return 0

    lax.fori_loop(0, CHUNKS, cross, 0)
    plan(0, ids_ref, scale_ref)

    def spread(k, kind, x):
        picked = jnp.dot(picks[kind], x, preferred_element_type=F32)
        send[k, kind] = picked.reshape(span, cap, w).astype(BF16)
        for d in range(1, span):
            remote(
                send.at[k, kind, d], recv.at[k, 4 * (span - d) + 2 * core + kind],
                send_sem.at[k], recv_sem.at[k], near_device(d, k % 2),
            ).start()
        mine = recv.at[k, 2 * core + kind]
        remote(send.at[k, kind, 0], mine, send_sem.at[k], pair_sem.at[k], partner).start()
        pltpu.make_async_copy(send.at[k, kind, 0], mine, own_sem.at[k]).start()

    def relay(k):
        spread(k, 0, tok_ref[:, columns(k)])
        arrived(raw.at[k], raw_recv.at[k])
        spread(k, 1, raw[k])

    def project(k):
        arrived(recv.at[k, pl.ds(2 * core, 2)], own_sem.at[k])
        arrived(recv.at[k, pl.ds(2 - 2 * core, 2)], pair_sem.at[k])
        x = recv[k].astype(F32).reshape(n_ep * cap, w).astype(BF16)
        depth = columns(k)
        gate_acc[...] += jnp.dot(x, wg[depth, :], preferred_element_type=F32)
        up_acc[...] += jnp.dot(x, wu[depth, :], preferred_element_type=F32)

    def consume(p):
        mine = 2 * p + core
        other = 2 * p + 1 - core
        direct = recv.at[mine, pl.ds(4, n_ep - 4)]
        arrived(direct, recv_sem.at[mine])
        remote(direct, direct, fwd_sem.at[p], recv_sem.at[mine], partner).start()
        project(mine)
        arrived(recv.at[other, pl.ds(4, n_ep - 4)], recv_sem.at[other])
        project(other)

    gate_acc[...] = jnp.zeros_like(gate_acc)
    up_acc[...] = jnp.zeros_like(up_acc)
    give_ids.wait_recv()
    give_scale.wait_recv()
    plan(1, far_ids, far_scale)
    relay(0)
    relay(1)
    give_d = remote(wd_hbm.at[0, :, pair_cols], wd.at[core], wd_sem.at[0], wd_sem.at[1], partner)
    give_d.start()
    load_g.wait()
    load_u.wait()

    def step(p, _):
        relay(2 * p)
        relay(2 * p + 1)
        consume(p - 1)
        return 0

    lax.fori_loop(1, per_core, step, 0)
    consume(per_core - 1)

    g = gate_acc[...]
    hid[core] = (g / (1.0 + jnp.exp(-g)) * up_acc[...]).astype(BF16)
    swap = remote(hid.at[core], hid.at[core], hid_sem.at[0], hid_sem.at[1], partner)
    swap.start()
    load_d.wait()
    arrived(wd.at[1 - core], wd_sem.at[1])
    arrived(hid.at[1 - core], hid_sem.at[1])

    def finish(j, _):
        cols = columns(j)
        y = jnp.dot(hid[0], wd[0, :, cols], preferred_element_type=F32)
        y += jnp.dot(hid[1], wd[1, :, cols], preferred_element_type=F32)
        ret[j] = y.reshape(n_ep, cap, w).astype(BF16)
        k = core * per_core + j
        for d in range(1, span):
            for b in range(2):
                remote(
                    ret.at[j, pl.ds(4 * d + 2 * b, 2)], res.at[k, span - d], ret_sem.at[j],
                    res_sem.at[k], near_device(d, b),
                ).start()
        remote(
            ret.at[j, pl.ds(2 - 2 * core, 2)], res.at[k, 0], ret_sem.at[j], res_sem.at[k], partner
        ).start()
        pltpu.make_async_copy(
            ret.at[j, pl.ds(2 * core, 2)], res.at[k, 0], res_sem.at[k]
        ).start()
        return 0

    lax.fori_loop(0, per_core, finish, 0)

    def chunk(i):
        return (i % 2) * per_core + i // 2

    def mixed(k, kind):
        y = res[k, :, kind].astype(F32).reshape(slots, w).astype(BF16)
        both = jnp.dot(mixes[kind], y, preferred_element_type=F32)
        return both[0:rows] + both[rows:]

    def gather(i, _):
        k = chunk(i)
        arrived(res.at[k], res_sem.at[k])
        far_out[k] = mixed(k, 1).astype(BF16)
        remote(far_out.at[k], far_in.at[k], far_send.at[k], far_recv.at[k], twin).start()
        near[k] = mixed(k, 0)
        return 0

    lax.fori_loop(0, CHUNKS, gather, 0)

    def combine(i, _):
        k = chunk(i)
        arrived(far_in.at[k], far_recv.at[k])
        out_ref[:, columns(k)] = (near[k] + far_in[k].astype(F32)).astype(BF16)
        arrived(raw.at[k], raw_send.at[k])
        arrived(send.at[k], send_sem.at[k])
        arrived(far_out.at[k], far_send.at[k])
        return 0

    lax.fori_loop(0, CHUNKS, combine, 0)

    def drain_pairs(j, _):
        mine = 2 * j + core
        arrived(recv.at[mine, pl.ds(4, n_ep - 4)], fwd_sem.at[j])
        arrived(ret.at[j, pl.ds(0, n_ep - 2)], ret_sem.at[j])
        return 0

    lax.fori_loop(0, per_core, drain_pairs, 0)
    swap.wait_send()
    give_d.wait_send()
    give_ids.wait_send()
    give_scale.wait_send()


def shards(tokens, expert_ids, gate_scale, gate_weight, up_weight, down_weight):
    rows, width = tokens.shape
    top = expert_ids.shape[1]
    n_ep = lax.axis_size("ep")
    experts = n_ep // 2
    span = experts // 2
    cap = 2 * (3 * rows * top // (4 * experts))
    cap = -(-cap // 8) * 8
    ff = gate_weight.shape[2]
    w = width // CHUNKS
    per_core = CHUNKS // 2
    vmem = pl.BlockSpec(memory_space=pltpu.VMEM)
    hbm = pl.BlockSpec(memory_space=pl.ANY)
    dma = pltpu.SemaphoreType.DMA
    total = n_ep * cap
    return pl.pallas_call(
        functools.partial(layer_kernel, n_ep, cap),
        out_shape=jax.ShapeDtypeStruct((rows, width), BF16),
        in_specs=[vmem, vmem, vmem, hbm, hbm, hbm],
        out_specs=vmem,
        scratch_shapes=[
            pltpu.VMEM((CHUNKS, 2, span, cap, w), BF16),
            pltpu.VMEM((CHUNKS, n_ep, cap, w), BF16),
            pltpu.VMEM((per_core, n_ep, cap, w), BF16),
            pltpu.VMEM((CHUNKS, span, 2, cap, w), BF16),
            pltpu.VMEM((CHUNKS, rows, w), BF16),
            pltpu.VMEM((CHUNKS, rows, w), BF16),
            pltpu.VMEM((CHUNKS, rows, w), BF16),
            pltpu.VMEM((CHUNKS, rows, w), F32),
            pltpu.VMEM((top, rows), jnp.int32),
            pltpu.VMEM((top, rows), F32),
            pltpu.VMEM((width, ff), BF16),
            pltpu.VMEM((width, ff), BF16),
            pltpu.VMEM((2, ff, width // 2), BF16),
            pltpu.VMEM((total, ff), F32),
            pltpu.VMEM((total, ff), F32),
            pltpu.VMEM((2, total, ff), BF16),
            pltpu.VMEM((2, span * cap, rows), BF16),
            pltpu.VMEM((2, 2 * rows, span * cap), BF16),
            dma((3,)),
            dma((2,)),
            dma((4,)),
            dma((CHUNKS,)),
            dma((CHUNKS,)),
            dma((CHUNKS,)),
            dma((CHUNKS,)),
            dma((CHUNKS,)),
            dma((CHUNKS,)),
            dma((per_core,)),
            dma((2,)),
            dma((per_core,)),
            dma((CHUNKS,)),
            dma((CHUNKS,)),
            dma((CHUNKS,)),
        ],
        compiler_params=pltpu.CompilerParams(
            collective_id=0, has_side_effects=True, vmem_limit_bytes=60 * 1024 * 1024
        ),
        cost_estimate=pl.CostEstimate(
            flops=6 * total * width * ff, bytes_accessed=6 * width * ff,
            transcendentals=total * ff,
        ),
    )(expert_ids.T, gate_scale.T, tokens, gate_weight, up_weight, down_weight)


def solution(mesh):
    in_specs = (
        P(("groups", "ep"), None),
        P(("groups", "ep"), None),
        P(("groups", "ep"), None),
        P("ep", None, None),
        P("ep", None, None),
        P("ep", None, None),
    )
    out_specs = P(("groups", "ep"), None)
    return jax.shard_map(shards, mesh=mesh, in_specs=in_specs, out_specs=out_specs, check_vma=False)
```

```python
import functools

import jax
import jax.numpy as jnp
from jax import lax
from jax.experimental import pallas as pl
from jax.experimental.pallas import tpu as pltpu
from jax.sharding import PartitionSpec as P

CHUNKS = 8
BF16, F32 = jnp.bfloat16, jnp.float32


def layer_kernel(
    n_ep, cap, ids_ref, scale_ref, tok_ref, wg_hbm, wu_hbm, wd_hbm, out_ref,
    send, recv, ret, res, raw, far_out, far_in, near, far_ids, far_scale,
    wg, wu, wd, gate_acc, up_acc, hid, picks, mixes,
    w_sem, wd_sem, meta_sem, raw_send, raw_recv, send_sem, own_sem, pair_sem, recv_sem,
    fwd_sem, hid_sem, ret_sem, res_sem, far_send, far_recv,
):
    me = lax.axis_index("ep")
    core = me % 2
    place = (me // 2) % (n_ep // 4)
    side = me // (n_ep // 2)
    span = n_ep // 4
    first = side * (n_ep // 2)
    partner = first + place * 2 + 1 - core
    twin = (1 - side) * (n_ep // 2) + lax.rem(place + span // 2, span) * 2 + core
    rows, width = tok_ref.shape
    w = width // CHUNKS
    per_core = CHUNKS // 2
    half = width // 2
    slots = span * cap

    def remote(src, dst, ssem, rsem, dev):
        return pltpu.make_async_remote_copy(
            src_ref=src, dst_ref=dst, send_sem=ssem, recv_sem=rsem,
            device_id={"ep": dev}, device_id_type=pl.DeviceIdType.MESH,
        )

    def near_device(d, b):
        return first + lax.rem(place + d, span) * 2 + b

    def columns(k):
        return pl.ds(pl.multiple_of(k * w, 128), w)

    def arrived(ref, sem):
        pltpu.make_async_copy(ref, ref, sem).wait()

    my_cols = pl.ds(pl.multiple_of(core * half, 128), half)
    pair_cols = pl.ds(pl.multiple_of((1 - core) * half, 128), half)
    load_g = pltpu.make_async_copy(wg_hbm.at[0], wg, w_sem.at[0])
    load_u = pltpu.make_async_copy(wu_hbm.at[0], wu, w_sem.at[1])
    load_d = pltpu.make_async_copy(wd_hbm.at[0, :, my_cols], wd.at[core], w_sem.at[2])
    load_g.start()
    load_u.start()
    load_d.start()

    barrier = pltpu.get_barrier_semaphore()
    for i in range(1, n_ep // 2):
        pl.semaphore_signal(
            barrier, inc=1, device_id={"ep": first + lax.rem(me + i, n_ep // 2)},
            device_id_type=pl.DeviceIdType.MESH,
        )
    pl.semaphore_signal(
        barrier, inc=1, device_id={"ep": twin}, device_id_type=pl.DeviceIdType.MESH
    )

    shape3 = (span, cap, rows)
    block = lax.broadcasted_iota(jnp.int32, shape3, 0).reshape(slots, rows)
    slot = lax.broadcasted_iota(jnp.int32, shape3, 1).reshape(slots, rows).astype(F32)
    named = place + block
    named = jnp.where(named >= span, named - span, named) + side * span
    r0 = lax.broadcasted_iota(jnp.int32, (rows, rows), 0)
    r1 = lax.broadcasted_iota(jnp.int32, (rows, rows), 1)
    earlier = jnp.where(r0 < r1, 1.0, 0.0).astype(BF16)
    unit = jnp.where(r0 == r1, 1.0, 0.0).astype(BF16)

    def plan(which, ids, scales):
        hit_a = ids[0:1, :] == named
        hit_b = ids[1:2, :] == named
        hit = jnp.where(hit_a | hit_b, 1.0, 0.0)
        before = jnp.dot(hit.astype(BF16), earlier, preferred_element_type=F32)
        hit = jnp.where(before == slot, hit, 0.0)
        picks[which] = hit.astype(BF16)
        scale = hit * jnp.where(hit_a, scales[0:1, :], scales[1:2, :])
        high = scale.astype(BF16)
        low = (scale - high.astype(F32)).astype(BF16)
        for i, term in enumerate((high, low)):
            mixes[which, i * rows:(i + 1) * rows] = lax.dot_general(
                unit, term, (((1,), (1,)), ((), ())), preferred_element_type=F32
            ).astype(BF16)

    pl.semaphore_wait(barrier, n_ep // 2)

    give_ids = remote(ids_ref, far_ids, meta_sem.at[0], meta_sem.at[1], twin)
    give_scale = remote(scale_ref, far_scale, meta_sem.at[2], meta_sem.at[3], twin)
    give_ids.start()
    give_scale.start()

    def cross(k, _):
        remote(tok_ref.at[:, columns(k)], raw.at[k], raw_send.at[k], raw_recv.at[k], twin).start()
        return 0

    lax.fori_loop(0, CHUNKS, cross, 0)
    plan(0, ids_ref, scale_ref)

    def spread(k, kind, x):
        picked = jnp.dot(picks[kind], x, preferred_element_type=F32)
        send[k, kind] = picked.reshape(span, cap, w).astype(BF16)
        for d in range(1, span):
            remote(
                send.at[k, kind, d], recv.at[k, 4 * (span - d) + 2 * core + kind],
                send_sem.at[k], recv_sem.at[k], near_device(d, k % 2),
            ).start()
        mine = recv.at[k, 2 * core + kind]
        remote(send.at[k, kind, 0], mine, send_sem.at[k], pair_sem.at[k], partner).start()
        pltpu.make_async_copy(send.at[k, kind, 0], mine, own_sem.at[k]).start()

    def relay(k):
        nxt = k + 2

        @pl.when(nxt < CHUNKS)
        def _():
            spread(nxt, 0, tok_ref[:, columns(nxt)])

        arrived(raw.at[k], raw_recv.at[k])
        spread(k, 1, raw[k])

    def project(k):
        arrived(recv.at[k, pl.ds(2 * core, 2)], own_sem.at[k])
        arrived(recv.at[k, pl.ds(2 - 2 * core, 2)], pair_sem.at[k])
        x = recv[k].astype(F32).reshape(n_ep * cap, w).astype(BF16)
        depth = columns(k)
        gate_acc[...] += jnp.dot(x, wg[depth, :], preferred_element_type=F32)
        up_acc[...] += jnp.dot(x, wu[depth, :], preferred_element_type=F32)

    def consume(p):
        mine = 2 * p + core
        other = 2 * p + 1 - core
        direct = recv.at[mine, pl.ds(4, n_ep - 4)]
        arrived(direct, recv_sem.at[mine])
        remote(direct, direct, fwd_sem.at[p], recv_sem.at[mine], partner).start()
        project(mine)
        arrived(recv.at[other, pl.ds(4, n_ep - 4)], recv_sem.at[other])
        project(other)

    gate_acc[...] = jnp.zeros_like(gate_acc)
    up_acc[...] = jnp.zeros_like(up_acc)
    spread(0, 0, tok_ref[:, columns(0)])
    spread(1, 0, tok_ref[:, columns(1)])
    give_ids.wait_recv()
    give_scale.wait_recv()
    plan(1, far_ids, far_scale)
    relay(0)
    relay(1)
    give_d = remote(wd_hbm.at[0, :, pair_cols], wd.at[core], wd_sem.at[0], wd_sem.at[1], partner)
    give_d.start()
    load_g.wait()
    load_u.wait()

    def step(p, _):
        relay(2 * p)
        relay(2 * p + 1)
        consume(p - 2)
        return 0

    relay(2)
    relay(3)
    lax.fori_loop(2, per_core, step, 0)
    consume(per_core - 2)
    consume(per_core - 1)

    g = gate_acc[...]
    hid[core] = (g / (1.0 + jnp.exp(-g)) * up_acc[...]).astype(BF16)
    swap = remote(hid.at[core], hid.at[core], hid_sem.at[0], hid_sem.at[1], partner)
    swap.start()
    load_d.wait()
    arrived(wd.at[1 - core], wd_sem.at[1])
    arrived(hid.at[1 - core], hid_sem.at[1])

    def finish(j, _):
        cols = columns(j)
        y = jnp.dot(hid[0], wd[0, :, cols], preferred_element_type=F32)
        y += jnp.dot(hid[1], wd[1, :, cols], preferred_element_type=F32)
        ret[j] = y.reshape(n_ep, cap, w).astype(BF16)
        k = core * per_core + j
        for d in range(1, span):
            for b in range(2):
                remote(
                    ret.at[j, pl.ds(4 * d + 2 * b, 2)], res.at[k, span - d], ret_sem.at[j],
                    res_sem.at[k], near_device(d, b),
                ).start()
        remote(
            ret.at[j, pl.ds(2 - 2 * core, 2)], res.at[k, 0], ret_sem.at[j], res_sem.at[k], partner
        ).start()
        pltpu.make_async_copy(
            ret.at[j, pl.ds(2 * core, 2)], res.at[k, 0], res_sem.at[k]
        ).start()
        return 0

    lax.fori_loop(0, per_core, finish, 0)

    def chunk(i):
        return (i % 2) * per_core + i // 2

    def mixed(k, kind):
        y = res[k, :, kind].astype(F32).reshape(slots, w).astype(BF16)
        both = jnp.dot(mixes[kind], y, preferred_element_type=F32)
        return both[0:rows] + both[rows:]

    def gather(i, _):
        k = chunk(i)
        arrived(res.at[k], res_sem.at[k])
        far_out[k] = mixed(k, 1).astype(BF16)
        remote(far_out.at[k], far_in.at[k], far_send.at[k], far_recv.at[k], twin).start()
        near[k] = mixed(k, 0)
        return 0

    lax.fori_loop(0, CHUNKS, gather, 0)

    def combine(i, _):
        k = chunk(i)
        arrived(far_in.at[k], far_recv.at[k])
        out_ref[:, columns(k)] = (near[k] + far_in[k].astype(F32)).astype(BF16)
        arrived(raw.at[k], raw_send.at[k])
        arrived(send.at[k], send_sem.at[k])
        arrived(far_out.at[k], far_send.at[k])
        return 0

    lax.fori_loop(0, CHUNKS, combine, 0)

    def drain_pairs(j, _):
        mine = 2 * j + core
        arrived(recv.at[mine, pl.ds(4, n_ep - 4)], fwd_sem.at[j])
        arrived(ret.at[j, pl.ds(0, n_ep - 2)], ret_sem.at[j])
        return 0

    lax.fori_loop(0, per_core, drain_pairs, 0)
    swap.wait_send()
    give_d.wait_send()
    give_ids.wait_send()
    give_scale.wait_send()


def shards(tokens, expert_ids, gate_scale, gate_weight, up_weight, down_weight):
    rows, width = tokens.shape
    top = expert_ids.shape[1]
    n_ep = lax.axis_size("ep")
    experts = n_ep // 2
    span = experts // 2
    cap = 2 * (3 * rows * top // (4 * experts))
    cap = -(-cap // 8) * 8
    ff = gate_weight.shape[2]
    w = width // CHUNKS
    per_core = CHUNKS // 2
    vmem = pl.BlockSpec(memory_space=pltpu.VMEM)
    hbm = pl.BlockSpec(memory_space=pl.ANY)
    dma = pltpu.SemaphoreType.DMA
    total = n_ep * cap
    return pl.pallas_call(
        functools.partial(layer_kernel, n_ep, cap),
        out_shape=jax.ShapeDtypeStruct((rows, width), BF16),
        in_specs=[vmem, vmem, vmem, hbm, hbm, hbm],
        out_specs=vmem,
        scratch_shapes=[
            pltpu.VMEM((CHUNKS, 2, span, cap, w), BF16),
            pltpu.VMEM((CHUNKS, n_ep, cap, w), BF16),
            pltpu.VMEM((per_core, n_ep, cap, w), BF16),
            pltpu.VMEM((CHUNKS, span, 2, cap, w), BF16),
            pltpu.VMEM((CHUNKS, rows, w), BF16),
            pltpu.VMEM((CHUNKS, rows, w), BF16),
            pltpu.VMEM((CHUNKS, rows, w), BF16),
            pltpu.VMEM((CHUNKS, rows, w), F32),
            pltpu.VMEM((top, rows), jnp.int32),
            pltpu.VMEM((top, rows), F32),
            pltpu.VMEM((width, ff), BF16),
            pltpu.VMEM((width, ff), BF16),
            pltpu.VMEM((2, ff, width // 2), BF16),
            pltpu.VMEM((total, ff), F32),
            pltpu.VMEM((total, ff), F32),
            pltpu.VMEM((2, total, ff), BF16),
            pltpu.VMEM((2, span * cap, rows), BF16),
            pltpu.VMEM((2, 2 * rows, span * cap), BF16),
            dma((3,)),
            dma((2,)),
            dma((4,)),
            dma((CHUNKS,)),
            dma((CHUNKS,)),
            dma((CHUNKS,)),
            dma((CHUNKS,)),
            dma((CHUNKS,)),
            dma((CHUNKS,)),
            dma((per_core,)),
            dma((2,)),
            dma((per_core,)),
            dma((CHUNKS,)),
            dma((CHUNKS,)),
            dma((CHUNKS,)),
        ],
        compiler_params=pltpu.CompilerParams(
            collective_id=0, has_side_effects=True, vmem_limit_bytes=60 * 1024 * 1024
        ),
        cost_estimate=pl.CostEstimate(
            flops=6 * total * width * ff, bytes_accessed=6 * width * ff,
            transcendentals=total * ff,
        ),
    )(expert_ids.T, gate_scale.T, tokens, gate_weight, up_weight, down_weight)


def solution(mesh):
    in_specs = (
        P(("groups", "ep"), None),
        P(("groups", "ep"), None),
        P(("groups", "ep"), None),
        P("ep", None, None),
        P("ep", None, None),
        P("ep", None, None),
    )
    out_specs = P(("groups", "ep"), None)
    return jax.shard_map(shards, mesh=mesh, in_specs=in_specs, out_specs=out_specs, check_vma=False)
```

```python
import functools

import jax
import jax.numpy as jnp
from jax import lax
from jax.experimental import pallas as pl
from jax.experimental.pallas import tpu as pltpu
from jax.sharding import PartitionSpec as P

CHUNKS = 8
BF16, F32 = jnp.bfloat16, jnp.float32


def layer_kernel(
    n_ep, cap, ids_ref, scale_ref, tok_ref, wg_hbm, wu_hbm, wd_hbm, out_ref,
    send, recv, ret, res, raw, far_out, far_in, near, far_ids, far_scale,
    wg, wu, wd, gate_acc, up_acc, hid, picks, mixes,
    w_sem, wd_sem, meta_sem, raw_send, raw_recv, send_sem, own_sem, pair_sem, recv_sem,
    fwd_sem, hid_sem, ret_sem, res_sem, far_send, far_recv,
):
    me = lax.axis_index("ep")
    core = me % 2
    place = (me // 2) % (n_ep // 4)
    side = me // (n_ep // 2)
    span = n_ep // 4
    first = side * (n_ep // 2)
    partner = first + place * 2 + 1 - core
    twin = (1 - side) * (n_ep // 2) + lax.rem(place + span // 2, span) * 2 + core
    rows, width = tok_ref.shape
    w = width // CHUNKS
    per_core = CHUNKS // 2
    half = width // 2
    slots = span * cap

    def remote(src, dst, ssem, rsem, dev):
        return pltpu.make_async_remote_copy(
            src_ref=src, dst_ref=dst, send_sem=ssem, recv_sem=rsem,
            device_id={"ep": dev}, device_id_type=pl.DeviceIdType.MESH,
        )

    def near_device(d, b):
        return first + lax.rem(place + d, span) * 2 + b

    def columns(k):
        return pl.ds(pl.multiple_of(k * w, 128), w)

    def arrived(ref, sem):
        pltpu.make_async_copy(ref, ref, sem).wait()

    my_cols = pl.ds(pl.multiple_of(core * half, 128), half)
    pair_cols = pl.ds(pl.multiple_of((1 - core) * half, 128), half)
    load_g = pltpu.make_async_copy(wg_hbm.at[0], wg, w_sem.at[0])
    load_u = pltpu.make_async_copy(wu_hbm.at[0], wu, w_sem.at[1])
    load_d = pltpu.make_async_copy(wd_hbm.at[0, :, my_cols], wd.at[core], w_sem.at[2])
    load_g.start()
    load_u.start()
    load_d.start()

    barrier = pltpu.get_barrier_semaphore()
    for i in range(1, n_ep // 2):
        pl.semaphore_signal(
            barrier, inc=1, device_id={"ep": first + lax.rem(me + i, n_ep // 2)},
            device_id_type=pl.DeviceIdType.MESH,
        )
    pl.semaphore_signal(
        barrier, inc=1, device_id={"ep": twin}, device_id_type=pl.DeviceIdType.MESH
    )

    shape3 = (span, cap, rows)
    block = lax.broadcasted_iota(jnp.int32, shape3, 0).reshape(slots, rows)
    slot = lax.broadcasted_iota(jnp.int32, shape3, 1).reshape(slots, rows).astype(F32)
    named = place + block
    named = jnp.where(named >= span, named - span, named) + side * span
    r0 = lax.broadcasted_iota(jnp.int32, (rows, rows), 0)
    r1 = lax.broadcasted_iota(jnp.int32, (rows, rows), 1)
    earlier = jnp.where(r0 < r1, 1.0, 0.0).astype(BF16)
    unit = jnp.where(r0 == r1, 1.0, 0.0).astype(BF16)

    def plan(which, ids, scales):
        hit_a = ids[0:1, :] == named
        hit_b = ids[1:2, :] == named
        hit = jnp.where(hit_a | hit_b, 1.0, 0.0)
        before = jnp.dot(hit.astype(BF16), earlier, preferred_element_type=F32)
        hit = jnp.where(before == slot, hit, 0.0)
        picks[which] = hit.astype(BF16)
        scale = hit * jnp.where(hit_a, scales[0:1, :], scales[1:2, :])
        high = scale.astype(BF16)
        low = (scale - high.astype(F32)).astype(BF16)
        for i, term in enumerate((high, low)):
            mixes[which, i * rows:(i + 1) * rows] = lax.dot_general(
                unit, term, (((1,), (1,)), ((), ())), preferred_element_type=F32
            ).astype(BF16)

    pl.semaphore_wait(barrier, n_ep // 2)

    give_ids = remote(ids_ref, far_ids, meta_sem.at[0], meta_sem.at[1], twin)
    give_scale = remote(scale_ref, far_scale, meta_sem.at[2], meta_sem.at[3], twin)
    give_ids.start()
    give_scale.start()

    def cross(k, _):
        remote(tok_ref.at[:, columns(k)], raw.at[k], raw_send.at[k], raw_recv.at[k], twin).start()
        return 0

    lax.fori_loop(0, CHUNKS, cross, 0)
    plan(0, ids_ref, scale_ref)

    def spread(k, kind, x):
        picked = jnp.dot(picks[kind], x, preferred_element_type=F32)
        send[k, kind] = picked.reshape(span, cap, w).astype(BF16)
        for d in range(1, span):
            remote(
                send.at[k, kind, d], recv.at[k, 4 * (span - d) + 2 * core + kind],
                send_sem.at[k], recv_sem.at[k], near_device(d, k % 2),
            ).start()
        mine = recv.at[k, 2 * core + kind]
        remote(send.at[k, kind, 0], mine, send_sem.at[k], pair_sem.at[k], partner).start()
        pltpu.make_async_copy(send.at[k, kind, 0], mine, own_sem.at[k]).start()

    def relay(k):
        nxt = k + 2

        @pl.when(nxt < CHUNKS)
        def _():
            spread(nxt, 0, tok_ref[:, columns(nxt)])

        arrived(raw.at[k], raw_recv.at[k])
        spread(k, 1, raw[k])

    def project(k):
        arrived(recv.at[k, pl.ds(2 * core, 2)], own_sem.at[k])
        arrived(recv.at[k, pl.ds(2 - 2 * core, 2)], pair_sem.at[k])
        x = recv[k].astype(F32).reshape(n_ep * cap, w).astype(BF16)
        depth = columns(k)
        gate_acc[...] += jnp.dot(x, wg[depth, :], preferred_element_type=F32)
        up_acc[...] += jnp.dot(x, wu[depth, :], preferred_element_type=F32)

    def consume(p):
        mine = 2 * p + core
        other = 2 * p + 1 - core
        direct = recv.at[mine, pl.ds(4, n_ep - 4)]
        arrived(direct, recv_sem.at[mine])
        remote(direct, direct, fwd_sem.at[p], recv_sem.at[mine], partner).start()
        project(mine)
        arrived(recv.at[other, pl.ds(4, n_ep - 4)], recv_sem.at[other])
        project(other)

    gate_acc[...] = jnp.zeros_like(gate_acc)
    up_acc[...] = jnp.zeros_like(up_acc)
    spread(0, 0, tok_ref[:, columns(0)])
    spread(1, 0, tok_ref[:, columns(1)])
    give_ids.wait_recv()
    give_scale.wait_recv()
    plan(1, far_ids, far_scale)
    relay(0)
    relay(1)
    give_d = remote(wd_hbm.at[0, :, pair_cols], wd.at[core], wd_sem.at[0], wd_sem.at[1], partner)
    give_d.start()
    load_g.wait()
    load_u.wait()

    def step(p, _):
        relay(2 * p)
        relay(2 * p + 1)
        consume(p - 2)
        return 0

    relay(2)
    relay(3)
    lax.fori_loop(2, per_core, step, 0)
    consume(per_core - 2)
    consume(per_core - 1)

    g = gate_acc[...]
    hid[core] = (g / (1.0 + jnp.exp(-g)) * up_acc[...]).astype(BF16)
    swap = remote(hid.at[core], hid.at[core], hid_sem.at[0], hid_sem.at[1], partner)
    swap.start()
    load_d.wait()
    arrived(wd.at[1 - core], wd_sem.at[1])
    arrived(hid.at[1 - core], hid_sem.at[1])

    def finish(j, _):
        cols = columns(j)
        y = jnp.dot(hid[0], wd[0, :, cols], preferred_element_type=F32)
        y += jnp.dot(hid[1], wd[1, :, cols], preferred_element_type=F32)
        ret[j] = y.reshape(n_ep, cap, w).astype(BF16)
        k = core * per_core + j
        for d in range(1, span):
            for b in range(2):
                remote(
                    ret.at[j, pl.ds(4 * d + 2 * b, 2)], res.at[k, span - d], ret_sem.at[j],
                    res_sem.at[k], near_device(d, b),
                ).start()
        remote(
            ret.at[j, pl.ds(2 - 2 * core, 2)], res.at[k, 0], ret_sem.at[j], res_sem.at[k], partner
        ).start()
        pltpu.make_async_copy(
            ret.at[j, pl.ds(2 * core, 2)], res.at[k, 0], res_sem.at[k]
        ).start()
        return 0

    lax.fori_loop(0, per_core, finish, 0)

    def chunk(i):
        return (i % 2) * per_core + i // 2

    def mixed(k, kind):
        y = res[k, :, kind].astype(F32).reshape(slots, w).astype(BF16)
        both = jnp.dot(mixes[kind], y, preferred_element_type=F32)
        return both[0:rows] + both[rows:]

    def gather(i, _):
        k = chunk(i)
        arrived(res.at[k], res_sem.at[k])
        far_out[k] = mixed(k, 1).astype(BF16)
        remote(far_out.at[k], far_in.at[k], far_send.at[k], far_recv.at[k], twin).start()
        near[k] = mixed(k, 0)
        return 0

    lax.fori_loop(0, per_core, gather, 0)

    def combine(i, _):
        k = chunk(i)
        arrived(far_in.at[k], far_recv.at[k])
        out_ref[:, columns(k)] = (near[k] + far_in[k].astype(F32)).astype(BF16)
        arrived(raw.at[k], raw_send.at[k])
        arrived(send.at[k], send_sem.at[k])
        arrived(far_out.at[k], far_send.at[k])
        return 0

    def overlap(i, _):
        gather(i, 0)
        return combine(i - per_core, 0)

    lax.fori_loop(per_core, CHUNKS, overlap, 0)
    lax.fori_loop(per_core, CHUNKS, combine, 0)

    def drain_pairs(j, _):
        mine = 2 * j + core
        arrived(recv.at[mine, pl.ds(4, n_ep - 4)], fwd_sem.at[j])
        arrived(ret.at[j, pl.ds(0, n_ep - 2)], ret_sem.at[j])
        return 0

    lax.fori_loop(0, per_core, drain_pairs, 0)
    swap.wait_send()
    give_d.wait_send()
    give_ids.wait_send()
    give_scale.wait_send()


def shards(tokens, expert_ids, gate_scale, gate_weight, up_weight, down_weight):
    rows, width = tokens.shape
    top = expert_ids.shape[1]
    n_ep = lax.axis_size("ep")
    experts = n_ep // 2
    span = experts // 2
    cap = 2 * (3 * rows * top // (4 * experts))
    cap = -(-cap // 8) * 8
    ff = gate_weight.shape[2]
    w = width // CHUNKS
    per_core = CHUNKS // 2
    vmem = pl.BlockSpec(memory_space=pltpu.VMEM)
    hbm = pl.BlockSpec(memory_space=pl.ANY)
    dma = pltpu.SemaphoreType.DMA
    total = n_ep * cap
    return pl.pallas_call(
        functools.partial(layer_kernel, n_ep, cap),
        out_shape=jax.ShapeDtypeStruct((rows, width), BF16),
        in_specs=[vmem, vmem, vmem, hbm, hbm, hbm],
        out_specs=vmem,
        scratch_shapes=[
            pltpu.VMEM((CHUNKS, 2, span, cap, w), BF16),
            pltpu.VMEM((CHUNKS, n_ep, cap, w), BF16),
            pltpu.VMEM((per_core, n_ep, cap, w), BF16),
            pltpu.VMEM((CHUNKS, span, 2, cap, w), BF16),
            pltpu.VMEM((CHUNKS, rows, w), BF16),
            pltpu.VMEM((CHUNKS, rows, w), BF16),
            pltpu.VMEM((CHUNKS, rows, w), BF16),
            pltpu.VMEM((CHUNKS, rows, w), F32),
            pltpu.VMEM((top, rows), jnp.int32),
            pltpu.VMEM((top, rows), F32),
            pltpu.VMEM((width, ff), BF16),
            pltpu.VMEM((width, ff), BF16),
            pltpu.VMEM((2, ff, width // 2), BF16),
            pltpu.VMEM((total, ff), F32),
            pltpu.VMEM((total, ff), F32),
            pltpu.VMEM((2, total, ff), BF16),
            pltpu.VMEM((2, span * cap, rows), BF16),
            pltpu.VMEM((2, 2 * rows, span * cap), BF16),
            dma((3,)),
            dma((2,)),
            dma((4,)),
            dma((CHUNKS,)),
            dma((CHUNKS,)),
            dma((CHUNKS,)),
            dma((CHUNKS,)),
            dma((CHUNKS,)),
            dma((CHUNKS,)),
            dma((per_core,)),
            dma((2,)),
            dma((per_core,)),
            dma((CHUNKS,)),
            dma((CHUNKS,)),
            dma((CHUNKS,)),
        ],
        compiler_params=pltpu.CompilerParams(
            collective_id=0, has_side_effects=True, vmem_limit_bytes=60 * 1024 * 1024
        ),
        cost_estimate=pl.CostEstimate(
            flops=6 * total * width * ff, bytes_accessed=6 * width * ff,
            transcendentals=total * ff,
        ),
    )(expert_ids.T, gate_scale.T, tokens, gate_weight, up_weight, down_weight)


def solution(mesh):
    in_specs = (
        P(("groups", "ep"), None),
        P(("groups", "ep"), None),
        P(("groups", "ep"), None),
        P("ep", None, None),
        P("ep", None, None),
        P("ep", None, None),
    )
    out_specs = P(("groups", "ep"), None)
    return jax.shard_map(shards, mesh=mesh, in_specs=in_specs, out_specs=out_specs, check_vma=False)
```
